32 devices in a mesh: groups: 2 (over x), row: 16 (over z, y, core).
Axes of the slice: x: 2, y: 2, z: 4, core: 2. Of those that a mesh axis runs over, the one named last changes fastest.
Arguments:
- design_rows: float32 [512, 8192], P(('groups', 'row')), parts along dimension 0, may hold values from -1.5 to 1.5
- arc_ids: int32 [512], P(('groups', 'row')), parts along dimension 0, may hold values from 0 to 3, never falling along the last dimension, each value on 1 to 128 neighbouring positions
- tile_order: int32 [64], replicated, may hold values from 0 to 63, each once
Outputs:
- normal_slab: float32 [5888, 8192], P('groups', 'row'), parts along dimension 0
The draws below stay inside these ranges and needn't reach their ends.
There are 2 independent parts, one for each index of `groups`. The reference program is written for one: setup_inputs(seed, part) draws one part's arguments, and reference() takes and returns one part's arrays. A program takes and returns all parts, laid end to end along the dimension named above; an argument that names none is the same for every part. Nothing has to cross between parts.
Inputs may be any that keep to these rules, and one draw needn't show every extreme that they name: `arc_ids`: arc ids never fall along the observations; each arc holds 1 to 128 consecutive observations, and some arc exactly 128. `tile_order`: each column tile appears once.
All inputs are finite; a program needn't handle non-finite values.
Results may differ from the reference program's by a relative error of at most 0.000086.
Values sent between devices are 32-bit elements; how exact they have to be, the bound alone decides.
A program may use at most 128 MiB of HBM per device.

```python
import math
import jax
import jax.numpy as jnp
import numpy as np
from jax import lax

SLAB = 2944
TILE = 128
ARC_MOST = 128
ARCS = 4
OBS = 256
NCOL = 8192
NT = 64


def levels(stream_key, dims, pieces, low, high):
    level, own = 1.0, jax.random.fold_in(stream_key, 6)
    for axis_at, shards_of in pieces:
        draws = jnp.exp(jax.random.uniform(jax.random.fold_in(own, axis_at), (shards_of,), jnp.float32, low / len(pieces), high / len(pieces)))
        level = level * jnp.repeat(draws, dims[axis_at] // shards_of).reshape([-1 if axis == axis_at else 1 for axis in range(len(dims))])
    return level


def profile(amount, total, most, skew):
    portions = [(1 << 20) // math.isqrt(rank ** skew) + 1 for rank in range(2, amount + 1)]
    surplus, counts = total - most - (amount - 1), [1] * (amount - 1)
    while surplus > 0:
        free = [i for i in range(amount - 1) if counts[i] < most]
        whole, left = sum([portions[i] for i in free]), surplus
        for i in free:
            extra = min(most - counts[i], max(1, left * portions[i] // whole), surplus)
            counts[i] = counts[i] + extra
            surplus = surplus - extra
    return np.array([most] + counts)


def uneven_parts(stream_key, number_of, total, most, skew):
    if number_of == 2:
        one = jax.random.randint(stream_key, (), max(1, total - most), min(most, total - 1) + 1)
        return jnp.stack([one, total - one])
    tallies = jnp.asarray(profile(number_of, total, most, skew), jnp.int32)
    couples = (number_of - 1) // 2
    source_of, receiver = tallies[1:1 + 2 * couples:2], tallies[2:2 + 2 * couples:2]
    slack = jnp.minimum(source_of - 1, most - receiver)
    passed = jax.random.randint(jax.random.fold_in(stream_key, 1), (couples,), 0, 1 << 20) % (slack + 1)
    tallies = tallies.at[1:1 + 2 * couples:2].set(source_of - passed).at[2:2 + 2 * couples:2].set(receiver + passed)
    return tallies[jax.random.permutation(jax.random.fold_in(stream_key, 2), number_of)]


def centred(rng, shape, spread, most, split=(), kind=jnp.bfloat16):
    result = jax.random.normal(rng, shape, jnp.float32) * spread
    if len(split) > 0:
        result = levels(rng, shape, split, -0.22, 0.18) * result
    return jnp.clip(result, min=-most, max=most).astype(kind)


def setup_inputs(seed: int = 0, part: int = 0) -> dict:
    key_list = jax.random.split(jax.random.key(seed), 4)
    own_keys = jax.random.split(jax.random.fold_in(key_list[3], part), 4)
    return {
        "design_rows": centred(own_keys[0], (OBS, NCOL), (OBS ** -0.25), 1.5, ((0, 16),), jnp.float32),
        "arc_ids": jnp.searchsorted(jnp.cumsum(uneven_parts(own_keys[1], ARCS, OBS, ARC_MOST, 0)), jnp.arange(OBS), side="right").astype(jnp.int32),
        "tile_order": jax.random.permutation(key_list[2], NT).astype(jnp.int32),
    }


def reference(design_rows, arc_ids, tile_order):
    ones = jnp.ones((OBS,), design_rows.dtype)
    arc_counts = jax.ops.segment_sum(ones, arc_ids, num_segments=ARCS)
    arc_sums = jax.ops.segment_sum(design_rows, arc_ids, num_segments=ARCS)
    arc_means = arc_sums / jnp.maximum(arc_counts, 1.0)[:, None]
    centered = design_rows - arc_means[arc_ids]
    owned = centered.reshape(OBS, NT, TILE)[:, tile_order, :].reshape(OBS, NCOL)
    return lax.dot_general(centered[:, :SLAB], owned, (((0,), (0,)), ((), ())),
                           precision=lax.Precision.HIGHEST, preferred_element_type=jnp.float32)
```

```python
import functools

import jax
import jax.numpy as jnp
from jax import lax
from jax.experimental import pallas as pl
from jax.experimental.pallas import tpu as pltpu
from jax.sharding import PartitionSpec as P

SLAB = 2944
TILE = 128
WIDE = SLAB + TILE
STEP = 384
CORES = 2
MESH = pl.DeviceIdType.MESH


def exchange(
    depth, order, ids, rows, slab_all, own_all,
    stage, packed, slab_recv, own_recv, slab_send, own_send, local_sem,
):
    me = lax.axis_index("row")
    n = lax.axis_size("row")
    obs = rows.shape[0]
    tiles = packed.shape[2] // TILE
    lane = depth * CORES
    layers = n // lane
    z, inner = me // lane, me % lane
    y, core = inner // CORES, inner % CORES

    barrier = pltpu.get_barrier_semaphore()

    @pl.loop(1, n)
    def _(hop):
        pl.semaphore_signal(
            barrier, inc=1, device_id={"row": lax.rem(me + hop, n)}, device_id_type=MESH
        )

    stage[:, :SLAB] = rows[:, :SLAB]
    for obs_at in range(obs):
        value = ids[obs_at].astype(jnp.float32)
        stage[obs_at : obs_at + 1, SLAB:] = jnp.full((1, TILE), value, jnp.float32)

    def at(layer, side, unit):
        return (layer * depth + side) * CORES + unit

    def pass_on(kind, origin, target, own=False):
        return pltpu.make_async_remote_copy(
            src_ref=stage if own else slab_all.at[origin],
            dst_ref=slab_all.at[origin],
            send_sem=slab_send.at[kind, origin],
            recv_sem=slab_recv.at[origin],
            device_id={"row": target},
            device_id_type=MESH,
        )

    up, down = at(z + 1, y, core), at(z - 1, y, core)
    across, twin = at(z, depth - 1 - y, core), at(z, y, CORES - 1 - core)

    def arrived(origin):
        pltpu.make_async_remote_copy(
            src_ref=stage, dst_ref=slab_all.at[origin], send_sem=slab_send.at[0, origin],
            recv_sem=slab_recv.at[origin], device_id={"row": twin}, device_id_type=MESH,
        ).wait_recv()

    pl.semaphore_wait(barrier, n - 1)

    @pl.when(z + 1 < layers)
    def _():
        pass_on(0, me, up, True).start()

    @pl.when(z > 0)
    def _():
        pass_on(1, me, down, True).start()

    if depth > 1:
        pass_on(2, me, across, True).start()
    pass_on(3, me, twin, True).start()
    keep = pltpu.make_async_copy(stage, slab_all.at[me], local_sem.at[0])
    keep.start()

    def pack(peer):
        for k in range(tiles):
            column = order[peer * tiles + k] * TILE
            packed[peer, :, k * TILE : (k + 1) * TILE] = rows[:, pl.ds(column, TILE)]

    def deal(peer):
        return pltpu.make_async_remote_copy(
            src_ref=packed.at[peer],
            dst_ref=own_all.at[me],
            send_sem=own_send.at[peer],
            recv_sem=own_recv.at[me],
            device_id={"row": peer},
            device_id_type=MESH,
        )

    @pl.loop(1, n)
    def _(hop):
        peer = lax.rem(me + hop, n)
        pack(peer)
        deal(peer).start()

    pack(me)
    keep_own = pltpu.make_async_copy(packed.at[me], own_all.at[me], local_sem.at[1])
    keep_own.start()

    @pl.loop(1, layers + 1)
    def _(s):
        @pl.when(z - s >= 0)
        def _():
            origin = at(z - s, y, core)
            arrived(origin)

            @pl.when(z + 1 < layers)
            def _():
                pass_on(0, origin, up).start()

            if depth > 1:
                pass_on(2, origin, across).start()
            pass_on(3, origin, twin).start()

        @pl.when(z + s < layers)
        def _():
            origin = at(z + s, y, core)
            arrived(origin)

            @pl.when(z > 0)
            def _():
                pass_on(1, origin, down).start()

            if depth > 1:
                pass_on(2, origin, across).start()
            pass_on(3, origin, twin).start()

        if depth > 1:
            @pl.when(z - s + 1 >= 0)
            def _():
                origin = at(z - s + 1, depth - 1 - y, core)
                arrived(origin)
                pass_on(3, origin, twin).start()

            @pl.when(jnp.logical_and(s > 1, z + s - 1 < layers))
            def _():
                origin = at(z + s - 1, depth - 1 - y, core)
                arrived(origin)
                pass_on(3, origin, twin).start()

    @pl.loop(0, layers)
    def _(layer):
        for side in range(depth):
            arrived(at(layer, side, CORES - 1 - core))

    @pl.loop(1, n)
    def _(hop):
        peer = lax.rem(me + hop, n)
        pltpu.make_async_remote_copy(
            src_ref=packed.at[peer], dst_ref=own_all.at[peer], send_sem=own_send.at[peer],
            recv_sem=own_recv.at[peer], device_id={"row": peer}, device_id_type=MESH,
        ).wait()

    keep.wait()
    keep_own.wait()

    @pl.loop(0, layers)
    def _(layer):
        origin = at(layer, y, core)

        @pl.when(jnp.logical_and(layer <= z, z + 1 < layers))
        def _():
            pass_on(0, origin, up).wait_send()

        @pl.when(jnp.logical_and(layer >= z, z > 0))
        def _():
            pass_on(1, origin, down).wait_send()

        if depth > 1:
            pass_on(2, origin, across).wait_send()
        for side in range(depth):
            pass_on(3, at(layer, side, core), twin).wait_send()


def two(value):
    high = value.astype(jnp.bfloat16)
    return high, (value - high.astype(jnp.float32)).astype(jnp.bfloat16)


def dot(left, right, over=1):
    return lax.dot_general(
        left, right, (((over,), (0,)), ((), ())), preferred_element_type=jnp.float32
    )


def normal(id_ref, own_ref, slab_ref, out_ref, same, counts, own_high, own_low):
    @pl.when(pl.program_id(0) == 0)
    def _():
        arcs = id_ref[...]
        across = jnp.transpose(arcs)[0:1, :]
        alike = (arcs[:, 0:1] == across).astype(jnp.float32)
        same[...] = alike.astype(jnp.bfloat16)
        counts[...] = jnp.broadcast_to(jnp.sum(alike, axis=1, keepdims=True), counts.shape)
        own = own_ref[...]
        high, rest = two(own)
        middle, low = two(own - high.astype(jnp.float32))
        mask = same[...]
        sums = dot(mask, low) + dot(mask, middle) + dot(mask, high)
        centered = own - sums / counts[:, 0:1]
        own_high[...], own_low[...] = two(centered)

    slab = slab_ref[...]
    shift = dot(same[...], slab.astype(jnp.bfloat16)) / counts[:, 0:1]
    high, low = two(jnp.transpose(slab - shift))
    out_ref[...] = dot(low, own_high[...]) + dot(high, own_low[...]) + dot(high, own_high[...])


def shards(depth, design_rows, arc_ids, tile_order):
    obs, columns = design_rows.shape
    n = lax.axis_size("row")
    mine = columns // n
    total = n * obs
    slab_all, own_all = pl.pallas_call(
        functools.partial(exchange, depth),
        out_shape=(
            jax.ShapeDtypeStruct((n, obs, WIDE), jnp.float32),
            jax.ShapeDtypeStruct((n, obs, mine), jnp.float32),
        ),
        in_specs=[
            pl.BlockSpec(memory_space=pltpu.SMEM),
            pl.BlockSpec(memory_space=pltpu.SMEM),
            pl.BlockSpec(memory_space=pltpu.VMEM),
        ],
        out_specs=(pl.BlockSpec(memory_space=pl.ANY), pl.BlockSpec(memory_space=pl.ANY)),
        scratch_shapes=[
            pltpu.VMEM((obs, WIDE), jnp.float32),
            pltpu.VMEM((n, obs, mine), jnp.float32),
            pltpu.SemaphoreType.DMA((n,)),
            pltpu.SemaphoreType.DMA((n,)),
            pltpu.SemaphoreType.DMA((4, n)),
            pltpu.SemaphoreType.DMA((n,)),
            pltpu.SemaphoreType.DMA((2,)),
        ],
        compiler_params=pltpu.CompilerParams(
            collective_id=0, has_side_effects=True, vmem_limit_bytes=16 << 20
        ),
        name="exchange",
    )(tile_order, arc_ids, design_rows)
    slab_all = slab_all.reshape(total, WIDE)
    own_all = own_all.reshape(total, mine)
    return pl.pallas_call(
        normal,
        grid=(pl.cdiv(SLAB, STEP),),
        out_shape=jax.ShapeDtypeStruct((SLAB, mine), jnp.float32),
        in_specs=[
            pl.BlockSpec((total, TILE), lambda i: (0, SLAB // TILE)),
            pl.BlockSpec((total, mine), lambda i: (0, 0)),
            pl.BlockSpec((total, STEP), lambda i: (0, i)),
        ],
        out_specs=pl.BlockSpec((STEP, mine), lambda i: (i, 0)),
        scratch_shapes=[
            pltpu.VMEM((total, total), jnp.bfloat16),
            pltpu.VMEM((total, TILE), jnp.float32),
            pltpu.VMEM((total, mine), jnp.bfloat16),
            pltpu.VMEM((total, mine), jnp.bfloat16),
        ],
        compiler_params=pltpu.CompilerParams(vmem_limit_bytes=40 << 20),
        name="normal",
    )(slab_all, own_all, slab_all)


def solution(mesh):
    depth = 4 // mesh.shape["groups"]
    return jax.shard_map(
        functools.partial(shards, depth),
        mesh=mesh,
        in_specs=(P(("groups", "row"), None), P(("groups", "row")), P()),
        out_specs=P("groups", "row"),
        check_vma=False,
    )
```

```python
import functools

import jax
import jax.numpy as jnp
from jax import lax
from jax.experimental import pallas as pl
from jax.experimental.pallas import tpu as pltpu
from jax.sharding import PartitionSpec as P

SLAB = 2944
TILE = 128
WIDE = SLAB + TILE
STEP = 768
PARTS = 2
DEALS = 2
CORES = 2
MESH = pl.DeviceIdType.MESH


def exchange(
    depth, order_in, ids_in, rows_in, slab_all, own_all,
    order, ids, rows, stage, packed, slab_recv, own_recv, slab_send, own_send, load_sem, keep_sem,
    in_below, in_above,
):
    me = lax.axis_index("row")
    n = lax.axis_size("row")
    obs = rows.shape[0]
    tiles = packed.shape[2] // TILE
    lane = depth * CORES
    layers = n // lane
    z, inner = me // lane, me % lane
    y, core = inner // CORES, inner % CORES
    halves, part = obs // 8, WIDE // PARTS
    pieces = halves * PARTS

    loads = [
        pltpu.make_async_copy(rows_in, rows, load_sem.at[0]),
        pltpu.make_async_copy(ids_in, ids, load_sem.at[1]),
        pltpu.make_async_copy(order_in, order, load_sem.at[2]),
    ]
    for load in loads:
        load.start()

    def at(layer, side, unit):
        return (layer * depth + side) * CORES + unit

    up, down = at(z + 1, y, core), at(z - 1, y, core)
    across, twin = at(z, depth - 1 - y, core), at(z, y, CORES - 1 - core)
    below, above = z > 0, z + 1 < layers

    def signal(semaphore, target):
        pl.semaphore_signal(semaphore, inc=1, device_id={"row": target}, device_id_type=MESH)

    barrier = pltpu.get_barrier_semaphore()

    @pl.loop(1, lane)
    def _(hop):
        signal(barrier, z * lane + (inner + hop) % lane)

    @pl.when(above)
    def _():
        signal(barrier, up)

    @pl.when(below)
    def _():
        signal(barrier, down)

    for load in loads:
        load.wait()
    stage[:, :SLAB] = rows[:, :SLAB]
    for obs_at in range(obs):
        value = ids[obs_at].astype(jnp.float32)
        stage[obs_at : obs_at + 1, SLAB:] = jnp.full((1, TILE), value, jnp.float32)

    def cut(ref, piece):
        return ref.at[pl.ds((piece // PARTS) * 8, 8), pl.ds((piece % PARTS) * part, part)]

    def pass_on(kind, origin, piece, target, own=False):
        return pltpu.make_async_remote_copy(
            src_ref=cut(stage if own else slab_all.at[origin], piece),
            dst_ref=cut(slab_all.at[origin], piece),
            send_sem=slab_send.at[kind, origin, piece],
            recv_sem=slab_recv.at[origin, piece],
            device_id={"row": target},
            device_id_type=MESH,
        )

    def arrived(origin, piece):
        pass_on(3, origin, piece, twin).wait_recv()

    def deal(peer):
        return pltpu.make_async_remote_copy(
            src_ref=packed.at[peer],
            dst_ref=own_all.at[me],
            send_sem=own_send.at[peer],
            recv_sem=own_recv.at[me],
            device_id={"row": peer},
            device_id_type=MESH,
        )

    def deals(layer):
        @pl.loop(0, lane)
        def _(unit):
            deal(layer * lane + unit).start()

    pl.semaphore_wait(barrier, lane - 1 + jnp.where(above, 1, 0) + jnp.where(below, 1, 0))

    @pl.when(above)
    def _():
        signal(in_below.at[z], up)

    @pl.when(below)
    def _():
        signal(in_above.at[z], down)

    for piece in range(pieces):
        @pl.when(z + 1 < layers)
        def _():
            pass_on(0, me, piece, up, True).start()

        @pl.when(z > 0)
        def _():
            pass_on(1, me, piece, down, True).start()

        if depth > 1:
            pass_on(2, me, piece, across, True).start()
        pass_on(3, me, piece, twin, True).start()
    keep = pltpu.make_async_copy(stage, slab_all.at[me], keep_sem.at[0])
    keep.start()

    @pl.loop(0, n)
    def _(peer):
        for k in range(tiles):
            column = order[peer * tiles + k] * TILE
            packed[peer, :, k * TILE : (k + 1) * TILE] = rows[:, pl.ds(column, TILE)]

    keep_own = pltpu.make_async_copy(packed.at[me], own_all.at[me], keep_sem.at[1])
    keep_own.start()

    @pl.loop(1, lane)
    def _(hop):
        deal(z * lane + (inner + hop) % lane).start()

    @pl.loop(1, layers)
    def _(s):
        @pl.when(z - s >= 0)
        def _():
            pl.semaphore_wait(in_below.at[z - s], 1)

            @pl.when(above)
            def _():
                signal(in_below.at[z - s], up)

        @pl.when(z + s < layers)
        def _():
            pl.semaphore_wait(in_above.at[z + s], 1)

            @pl.when(below)
            def _():
                signal(in_above.at[z + s], down)

        if DEALS == 1:
            @pl.when(z - s >= 0)
            def _():
                deals(z - s)

            @pl.when(z + s < layers)
            def _():
                deals(z + s)

        for piece in range(pieces):
            @pl.when(z - s >= 0)
            def _():
                origin = at(z - s, y, core)
                arrived(origin, piece)

                @pl.when(z + 1 < layers)
                def _():
                    pass_on(0, origin, piece, up).start()

                if depth > 1:
                    pass_on(2, origin, piece, across).start()
                pass_on(3, origin, piece, twin).start()

            @pl.when(z + s < layers)
            def _():
                origin = at(z + s, y, core)
                arrived(origin, piece)

                @pl.when(z > 0)
                def _():
                    pass_on(1, origin, piece, down).start()

                if depth > 1:
                    pass_on(2, origin, piece, across).start()
                pass_on(3, origin, piece, twin).start()

        if DEALS == 2:
            @pl.when(z - s >= 0)
            def _():
                deals(z - s)

            @pl.when(z + s < layers)
            def _():
                deals(z + s)

    if DEALS == 3:
        @pl.loop(1, layers)
        def _(s):
            @pl.when(z - s >= 0)
            def _():
                deals(z - s)

            @pl.when(z + s < layers)
            def _():
                deals(z + s)

    if depth > 1:
        @pl.loop(1, layers + 1)
        def _(s):
            for piece in range(pieces):
                @pl.when(z - s + 1 >= 0)
                def _():
                    origin = at(z - s + 1, depth - 1 - y, core)
                    arrived(origin, piece)
                    pass_on(3, origin, piece, twin).start()

                @pl.when(jnp.logical_and(s > 1, z + s - 1 < layers))
                def _():
                    origin = at(z + s - 1, depth - 1 - y, core)
                    arrived(origin, piece)
                    pass_on(3, origin, piece, twin).start()

    @pl.loop(0, layers)
    def _(layer):
        for side in range(depth):
            for piece in range(pieces):
                arrived(at(layer, side, CORES - 1 - core), piece)

    @pl.loop(1, n)
    def _(hop):
        peer = lax.rem(me + hop, n)
        pltpu.make_async_remote_copy(
            src_ref=packed.at[peer], dst_ref=own_all.at[peer], send_sem=own_send.at[peer],
            recv_sem=own_recv.at[peer], device_id={"row": peer}, device_id_type=MESH,
        ).wait()

    keep.wait()
    keep_own.wait()

    @pl.loop(0, layers)
    def _(layer):
        origin = at(layer, y, core)
        for piece in range(pieces):
            @pl.when(jnp.logical_and(layer <= z, z + 1 < layers))
            def _():
                pass_on(0, origin, piece, up).wait_send()

            @pl.when(jnp.logical_and(layer >= z, z > 0))
            def _():
                pass_on(1, origin, piece, down).wait_send()

            if depth > 1:
                pass_on(2, origin, piece, across).wait_send()
            for side in range(depth):
                pass_on(3, at(layer, side, core), piece, twin).wait_send()


def two(value):
    high = value.astype(jnp.bfloat16)
    return high, (value - high.astype(jnp.float32)).astype(jnp.bfloat16)


def dot(left, right, over=1):
    return lax.dot_general(
        left, right, (((over,), (0,)), ((), ())), preferred_element_type=jnp.float32
    )


def normal(id_ref, own_ref, slab_ref, out_ref, average, own_parts):
    total = own_ref.shape[0]

    @pl.when(pl.program_id(0) == 0)
    def _():
        arcs = id_ref[...]
        alike = (arcs[:, 0:1] == jnp.transpose(arcs)[0:1, :]).astype(jnp.float32)
        counts = jnp.sum(alike, axis=1, keepdims=True)
        average[...] = (alike / counts).astype(jnp.bfloat16)
        mask = alike.astype(jnp.bfloat16)
        own = own_ref[...]
        high, rest = two(own)
        middle, low = two(own - high.astype(jnp.float32))
        sums = dot(mask, low) + dot(mask, middle) + dot(mask, high)
        centered = own - sums / counts
        high, low = two(centered)
        own_parts[:total], own_parts[total : 2 * total], own_parts[2 * total :] = high, low, high

    slab = slab_ref[...]
    high, low = two(jnp.transpose(slab - dot(average[...], slab.astype(jnp.bfloat16))))
    out_ref[...] = dot(jnp.concatenate([low, high, high], axis=1), own_parts[...])


def shards(depth, design_rows, arc_ids, tile_order):
    obs, columns = design_rows.shape
    n = lax.axis_size("row")
    mine = columns // n
    total = n * obs
    pieces = obs // 8 * PARTS
    layers = n // (depth * CORES)
    slab_all, own_all = pl.pallas_call(
        functools.partial(exchange, depth),
        out_shape=(
            jax.ShapeDtypeStruct((n, obs, WIDE), jnp.float32),
            jax.ShapeDtypeStruct((n, obs, mine), jnp.float32),
        ),
        in_specs=[
            pl.BlockSpec(memory_space=pltpu.HBM),
            pl.BlockSpec(memory_space=pltpu.HBM),
            pl.BlockSpec(memory_space=pltpu.HBM),
        ],
        out_specs=(pl.BlockSpec(memory_space=pl.ANY), pl.BlockSpec(memory_space=pl.ANY)),
        scratch_shapes=[
            pltpu.SMEM(tile_order.shape, jnp.int32),
            pltpu.SMEM(arc_ids.shape, jnp.int32),
            pltpu.VMEM(design_rows.shape, jnp.float32),
            pltpu.VMEM((obs, WIDE), jnp.float32),
            pltpu.VMEM((n, obs, mine), jnp.float32),
            pltpu.SemaphoreType.DMA((n, pieces)),
            pltpu.SemaphoreType.DMA((n,)),
            pltpu.SemaphoreType.DMA((4, n, pieces)),
            pltpu.SemaphoreType.DMA((n,)),
            pltpu.SemaphoreType.DMA((3,)),
            pltpu.SemaphoreType.DMA((2,)),
            pltpu.SemaphoreType.REGULAR((layers,)),
            pltpu.SemaphoreType.REGULAR((layers,)),
        ],
        compiler_params=pltpu.CompilerParams(
            collective_id=0, has_side_effects=True, vmem_limit_bytes=60 << 20
        ),
        name="exchange",
    )(tile_order, arc_ids, design_rows)
    slab_all = slab_all.reshape(total, WIDE)
    own_all = own_all.reshape(total, mine)
    return pl.pallas_call(
        normal,
        grid=(pl.cdiv(SLAB, STEP),),
        out_shape=jax.ShapeDtypeStruct((SLAB, mine), jnp.float32),
        in_specs=[
            pl.BlockSpec((total, TILE), lambda i: (0, SLAB // TILE)),
            pl.BlockSpec((total, mine), lambda i: (0, 0)),
            pl.BlockSpec((total, STEP), lambda i: (0, i)),
        ],
        out_specs=pl.BlockSpec((STEP, mine), lambda i: (i, 0)),
        scratch_shapes=[
            pltpu.VMEM((total, total), jnp.bfloat16),
            pltpu.VMEM((3 * total, mine), jnp.bfloat16),
        ],
        compiler_params=pltpu.CompilerParams(vmem_limit_bytes=60 << 20),
        name="normal",
    )(slab_all, own_all, slab_all)


def solution(mesh):
    depth = 4 // mesh.shape["groups"]
    return jax.shard_map(
        functools.partial(shards, depth),
        mesh=mesh,
        in_specs=(P(("groups", "row"), None), P(("groups", "row")), P()),
        out_specs=P("groups", "row"),
        check_vma=False,
    )
```

```python
import functools

import jax
import jax.numpy as jnp
from jax import lax
from jax.experimental import pallas as pl
from jax.experimental.pallas import tpu as pltpu
from jax.sharding import PartitionSpec as P

SLAB = 2944
TILE = 128
WIDE = SLAB + TILE
STEP = 1024
PARTS = 1
ROWS = 8
DEALS = 2
CORES = 2
MESH = pl.DeviceIdType.MESH


def exchange(
    depth, order_in, ids_in, rows_in, slab_all, own_all,
    order, ids, rows, stage, packed, slab_recv, own_recv, slab_send, own_send, load_sem, keep_sem,
    in_below, in_above,
):
    me = lax.axis_index("row")
    n = lax.axis_size("row")
    obs = rows.shape[0]
    tiles = packed.shape[2] // TILE
    lane = depth * CORES
    layers = n // lane
    z, inner = me // lane, me % lane
    y, core = inner // CORES, inner % CORES
    halves, part = obs // ROWS, WIDE // PARTS
    pieces = halves * PARTS

    loads = [
        pltpu.make_async_copy(rows_in, rows, load_sem.at[0]),
        pltpu.make_async_copy(ids_in, ids, load_sem.at[1]),
        pltpu.make_async_copy(order_in, order, load_sem.at[2]),
    ]
    for load in loads:
        load.start()

    def at(layer, side, unit):
        return (layer * depth + side) * CORES + unit

    up, down = at(z + 1, y, core), at(z - 1, y, core)
    across, twin = at(z, depth - 1 - y, core), at(z, y, CORES - 1 - core)
    below, above = z > 0, z + 1 < layers

    def signal(semaphore, target):
        pl.semaphore_signal(semaphore, inc=1, device_id={"row": target}, device_id_type=MESH)

    barrier = pltpu.get_barrier_semaphore()

    @pl.loop(1, lane)
    def _(hop):
        signal(barrier, z * lane + (inner + hop) % lane)

    @pl.when(above)
    def _():
        signal(barrier, up)

    @pl.when(below)
    def _():
        signal(barrier, down)

    for load in loads:
        load.wait()
    stage[:, :SLAB] = rows[:, :SLAB]
    for obs_at in range(obs):
        value = ids[obs_at].astype(jnp.float32)
        stage[obs_at : obs_at + 1, SLAB:] = jnp.full((1, TILE), value, jnp.float32)

    def cut(ref, piece):
        return ref.at[pl.ds((piece // PARTS) * ROWS, ROWS), pl.ds((piece % PARTS) * part, part)]

    def pass_on(kind, origin, piece, target, own=False):
        return pltpu.make_async_remote_copy(
            src_ref=cut(stage if own else slab_all.at[origin], piece),
            dst_ref=cut(slab_all.at[origin], piece),
            send_sem=slab_send.at[kind, origin, piece],
            recv_sem=slab_recv.at[origin, piece],
            device_id={"row": target},
            device_id_type=MESH,
        )

    def arrived(origin, piece):
        pass_on(3, origin, piece, twin).wait_recv()

    def deal(peer):
        return pltpu.make_async_remote_copy(
            src_ref=packed.at[peer],
            dst_ref=own_all.at[me],
            send_sem=own_send.at[peer],
            recv_sem=own_recv.at[me],
            device_id={"row": peer},
            device_id_type=MESH,
        )

    def deals(layer):
        @pl.loop(0, lane)
        def _(unit):
            deal(layer * lane + unit).start()

    pl.semaphore_wait(barrier, lane - 1 + jnp.where(above, 1, 0) + jnp.where(below, 1, 0))

    @pl.when(above)
    def _():
        signal(in_below.at[z], up)

    @pl.when(below)
    def _():
        signal(in_above.at[z], down)

    for piece in range(pieces):
        @pl.when(z + 1 < layers)
        def _():
            pass_on(0, me, piece, up, True).start()

        @pl.when(z > 0)
        def _():
            pass_on(1, me, piece, down, True).start()

        if depth > 1:
            pass_on(2, me, piece, across, True).start()
        pass_on(3, me, piece, twin, True).start()
    keep = pltpu.make_async_copy(stage, slab_all.at[me], keep_sem.at[0])
    keep.start()

    @pl.loop(0, n)
    def _(peer):
        for k in range(tiles):
            column = order[peer * tiles + k] * TILE
            packed[peer, :, k * TILE : (k + 1) * TILE] = rows[:, pl.ds(column, TILE)]

    keep_own = pltpu.make_async_copy(packed.at[me], own_all.at[me], keep_sem.at[1])
    keep_own.start()

    @pl.loop(1, lane)
    def _(hop):
        deal(z * lane + (inner + hop) % lane).start()

    @pl.loop(1, layers)
    def _(s):
        @pl.when(z - s >= 0)
        def _():
            pl.semaphore_wait(in_below.at[z - s], 1)

            @pl.when(above)
            def _():
                signal(in_below.at[z - s], up)

        @pl.when(z + s < layers)
        def _():
            pl.semaphore_wait(in_above.at[z + s], 1)

            @pl.when(below)
            def _():
                signal(in_above.at[z + s], down)

        if DEALS == 1:
            @pl.when(z - s >= 0)
            def _():
                deals(z - s)

            @pl.when(z + s < layers)
            def _():
                deals(z + s)

        for piece in range(pieces):
            @pl.when(z - s >= 0)
            def _():
                origin = at(z - s, y, core)
                arrived(origin, piece)

                @pl.when(z + 1 < layers)
                def _():
                    pass_on(0, origin, piece, up).start()

                if depth > 1:
                    pass_on(2, origin, piece, across).start()
                pass_on(3, origin, piece, twin).start()

            @pl.when(z + s < layers)
            def _():
                origin = at(z + s, y, core)
                arrived(origin, piece)

                @pl.when(z > 0)
                def _():
                    pass_on(1, origin, piece, down).start()

                if depth > 1:
                    pass_on(2, origin, piece, across).start()
                pass_on(3, origin, piece, twin).start()

        if DEALS == 2:
            @pl.when(z - s >= 0)
            def _():
                deals(z - s)

            @pl.when(z + s < layers)
            def _():
                deals(z + s)

    if DEALS == 3:
        @pl.loop(1, layers)
        def _(s):
            @pl.when(z - s >= 0)
            def _():
                deals(z - s)

            @pl.when(z + s < layers)
            def _():
                deals(z + s)

    if depth > 1:
        @pl.loop(1, layers + 1)
        def _(s):
            for piece in range(pieces):
                @pl.when(z - s + 1 >= 0)
                def _():
                    origin = at(z - s + 1, depth - 1 - y, core)
                    arrived(origin, piece)
                    pass_on(3, origin, piece, twin).start()

                @pl.when(jnp.logical_and(s > 1, z + s - 1 < layers))
                def _():
                    origin = at(z + s - 1, depth - 1 - y, core)
                    arrived(origin, piece)
                    pass_on(3, origin, piece, twin).start()

    @pl.loop(0, layers)
    def _(layer):
        for side in range(depth):
            for piece in range(pieces):
                arrived(at(layer, side, CORES - 1 - core), piece)

    @pl.loop(1, n)
    def _(hop):
        peer = lax.rem(me + hop, n)
        pltpu.make_async_remote_copy(
            src_ref=packed.at[peer], dst_ref=own_all.at[peer], send_sem=own_send.at[peer],
            recv_sem=own_recv.at[peer], device_id={"row": peer}, device_id_type=MESH,
        ).wait()

    keep.wait()
    keep_own.wait()

    @pl.loop(0, layers)
    def _(layer):
        origin = at(layer, y, core)
        for piece in range(pieces):
            @pl.when(jnp.logical_and(layer <= z, z + 1 < layers))
            def _():
                pass_on(0, origin, piece, up).wait_send()

            @pl.when(jnp.logical_and(layer >= z, z > 0))
            def _():
                pass_on(1, origin, piece, down).wait_send()

            if depth > 1:
                pass_on(2, origin, piece, across).wait_send()
            for side in range(depth):
                pass_on(3, at(layer, side, core), piece, twin).wait_send()


def two(value):
    high = value.astype(jnp.bfloat16)
    return high, (value - high.astype(jnp.float32)).astype(jnp.bfloat16)


def dot(left, right, over=1):
    return lax.dot_general(
        left, right, (((over,), (0,)), ((), ())), preferred_element_type=jnp.float32
    )


def normal(slab_in, own_in, out_ref, arcs_buf, own_buf, slab_buf, out_buf, average, own_parts, in_sem, out_sem):
    total = own_in.shape[0]
    spans = [(at, min(STEP, SLAB - at)) for at in range(0, SLAB, STEP)]

    def load(step):
        at, wide = spans[step]
        columns = pl.ds(at, wide)
        return pltpu.make_async_copy(slab_in.at[:, columns], slab_buf.at[:, columns], in_sem.at[2 + step])

    def store(step):
        at, wide = spans[step]
        columns = pl.ds(at, wide)
        return pltpu.make_async_copy(out_buf.at[columns], out_ref.at[columns], out_sem.at[step])

    load_arcs = pltpu.make_async_copy(slab_in.at[:, pl.ds(SLAB, TILE)], arcs_buf, in_sem.at[0])
    load_own = pltpu.make_async_copy(own_in, own_buf, in_sem.at[1])
    load_arcs.start()
    load_own.start()
    for step in range(len(spans)):
        load(step).start()

    load_arcs.wait()
    arcs = arcs_buf[...]
    alike = (arcs[:, 0:1] == jnp.transpose(arcs)[0:1, :]).astype(jnp.float32)
    counts = jnp.sum(alike, axis=1, keepdims=True)
    average[...] = (alike / counts).astype(jnp.bfloat16)
    mask = alike.astype(jnp.bfloat16)
    load_own.wait()
    own = own_buf[...]
    high = own.astype(jnp.bfloat16)
    middle, low = two(own - high.astype(jnp.float32))
    sums = dot(mask, low) + dot(mask, middle) + dot(mask, high)
    high, low = two(own - sums / counts)
    own_parts[:total], own_parts[total : 2 * total], own_parts[2 * total :] = high, low, high

    for step, (at, wide) in enumerate(spans):
        load(step).wait()
        slab = slab_buf[:, at : at + wide]
        high, low = two(jnp.transpose(slab - dot(average[...], slab.astype(jnp.bfloat16))))
        out_buf[at : at + wide] = dot(jnp.concatenate([low, high, high], axis=1), own_parts[...])
        store(step).start()

    for step in range(len(spans)):
        store(step).wait()


def shards(depth, design_rows, arc_ids, tile_order):
    obs, columns = design_rows.shape
    n = lax.axis_size("row")
    mine = columns // n
    total = n * obs
    pieces = obs // ROWS * PARTS
    layers = n // (depth * CORES)
    slab_all, own_all = pl.pallas_call(
        functools.partial(exchange, depth),
        out_shape=(
            jax.ShapeDtypeStruct((n, obs, WIDE), jnp.float32),
            jax.ShapeDtypeStruct((n, obs, mine), jnp.float32),
        ),
        in_specs=[
            pl.BlockSpec(memory_space=pltpu.HBM),
            pl.BlockSpec(memory_space=pltpu.HBM),
            pl.BlockSpec(memory_space=pltpu.HBM),
        ],
        out_specs=(pl.BlockSpec(memory_space=pl.ANY), pl.BlockSpec(memory_space=pl.ANY)),
        scratch_shapes=[
            pltpu.SMEM(tile_order.shape, jnp.int32),
            pltpu.SMEM(arc_ids.shape, jnp.int32),
            pltpu.VMEM(design_rows.shape, jnp.float32),
            pltpu.VMEM((obs, WIDE), jnp.float32),
            pltpu.VMEM((n, obs, mine), jnp.float32),
            pltpu.SemaphoreType.DMA((n, pieces)),
            pltpu.SemaphoreType.DMA((n,)),
            pltpu.SemaphoreType.DMA((4, n, pieces)),
            pltpu.SemaphoreType.DMA((n,)),
            pltpu.SemaphoreType.DMA((3,)),
            pltpu.SemaphoreType.DMA((2,)),
            pltpu.SemaphoreType.REGULAR((layers,)),
            pltpu.SemaphoreType.REGULAR((layers,)),
        ],
        compiler_params=pltpu.CompilerParams(
            collective_id=0, has_side_effects=True, vmem_limit_bytes=60 << 20
        ),
        name="exchange",
    )(tile_order, arc_ids, design_rows)
    slab_all = slab_all.reshape(total, WIDE)
    own_all = own_all.reshape(total, mine)
    steps = pl.cdiv(SLAB, STEP)
    return pl.pallas_call(
        normal,
        out_shape=jax.ShapeDtypeStruct((SLAB, mine), jnp.float32),
        in_specs=[pl.BlockSpec(memory_space=pl.ANY), pl.BlockSpec(memory_space=pl.ANY)],
        out_specs=pl.BlockSpec(memory_space=pl.ANY),
        scratch_shapes=[
            pltpu.VMEM((total, TILE), jnp.float32),
            pltpu.VMEM((total, mine), jnp.float32),
            pltpu.VMEM((total, SLAB), jnp.float32),
            pltpu.VMEM((SLAB, mine), jnp.float32),
            pltpu.VMEM((total, total), jnp.bfloat16),
            pltpu.VMEM((3 * total, mine), jnp.bfloat16),
            pltpu.SemaphoreType.DMA((2 + steps,)),
            pltpu.SemaphoreType.DMA((steps,)),
        ],
        compiler_params=pltpu.CompilerParams(vmem_limit_bytes=60 << 20),
        name="normal",
    )(slab_all, own_all)


def solution(mesh):
    depth = 4 // mesh.shape["groups"]
    return jax.shard_map(
        functools.partial(shards, depth),
        mesh=mesh,
        in_specs=(P(("groups", "row"), None), P(("groups", "row")), P()),
        out_specs=P("groups", "row"),
        check_vma=False,
    )
```

```python
import functools

import jax
import jax.numpy as jnp
from jax import lax
from jax.experimental import pallas as pl
from jax.experimental.pallas import tpu as pltpu
from jax.sharding import PartitionSpec as P

SLAB = 2944
TILE = 128
WIDE = SLAB + TILE
STEP = 1024
PARTS = 1
ROWS = 8
CORES = 2
MESH = pl.DeviceIdType.MESH


def exchange(
    depth, order_in, ids_in, rows_in, slab_all, own_all,
    order, ids, rows, stage, packed, slab_recv, own_recv, slab_send, own_send, load_sem, keep_sem,
    in_below, in_above,
):
    me = lax.axis_index("row")
    n = lax.axis_size("row")
    obs = rows.shape[0]
    tiles = packed.shape[2] // TILE
    lane = depth * CORES
    layers = n // lane
    z, inner = me // lane, me % lane
    y, core = inner // CORES, inner % CORES
    halves, part = obs // ROWS, WIDE // PARTS
    pieces = halves * PARTS

    loads = [
        pltpu.make_async_copy(rows_in, rows, load_sem.at[0]),
        pltpu.make_async_copy(ids_in, ids, load_sem.at[1]),
        pltpu.make_async_copy(order_in, order, load_sem.at[2]),
    ]
    for load in loads:
        load.start()

    def at(layer, side, unit):
        return (layer * depth + side) * CORES + unit

    up, down = at(z + 1, y, core), at(z - 1, y, core)
    across, twin = at(z, depth - 1 - y, core), at(z, y, CORES - 1 - core)
    below, above = z > 0, z + 1 < layers

    def signal(semaphore, target):
        pl.semaphore_signal(semaphore, inc=1, device_id={"row": target}, device_id_type=MESH)

    barrier = pltpu.get_barrier_semaphore()

    @pl.loop(1, lane)
    def _(hop):
        signal(barrier, z * lane + (inner + hop) % lane)

    @pl.when(above)
    def _():
        signal(barrier, up)

    @pl.when(below)
    def _():
        signal(barrier, down)

    for load in loads:
        load.wait()
    stage[:, :SLAB] = rows[:, :SLAB]
    for obs_at in range(obs):
        value = ids[obs_at].astype(jnp.float32)
        stage[obs_at : obs_at + 1, SLAB:] = jnp.full((1, TILE), value, jnp.float32)

    def cut(ref, piece):
        return ref.at[pl.ds((piece // PARTS) * ROWS, ROWS), pl.ds((piece % PARTS) * part, part)]

    def pass_on(kind, origin, piece, target, own=False):
        return pltpu.make_async_remote_copy(
            src_ref=cut(stage if own else slab_all.at[origin], piece),
            dst_ref=cut(slab_all.at[origin], piece),
            send_sem=slab_send.at[kind, origin, piece],
            recv_sem=slab_recv.at[origin, piece],
            device_id={"row": target},
            device_id_type=MESH,
        )

    def arrived(origin, piece):
        pass_on(3, origin, piece, twin).wait_recv()

    def deal(peer):
        return pltpu.make_async_remote_copy(
            src_ref=packed.at[peer],
            dst_ref=own_all.at[me],
            send_sem=own_send.at[peer],
            recv_sem=own_recv.at[me],
            device_id={"row": peer},
            device_id_type=MESH,
        )

    def deals(layer):
        @pl.loop(0, lane)
        def _(unit):
            deal(layer * lane + unit).start()

    pl.semaphore_wait(barrier, lane - 1 + jnp.where(above, 1, 0) + jnp.where(below, 1, 0))

    @pl.when(above)
    def _():
        signal(in_below.at[z], up)

    @pl.when(below)
    def _():
        signal(in_above.at[z], down)

    for piece in range(pieces):
        @pl.when(z + 1 < layers)
        def _():
            pass_on(0, me, piece, up, True).start()

        @pl.when(z > 0)
        def _():
            pass_on(1, me, piece, down, True).start()

        if depth > 1:
            pass_on(2, me, piece, across, True).start()
        pass_on(3, me, piece, twin, True).start()
    keep = pltpu.make_async_copy(stage, slab_all.at[me], keep_sem.at[0])
    keep.start()

    @pl.loop(0, n)
    def _(peer):
        for k in range(tiles):
            column = order[peer * tiles + k] * TILE
            packed[peer, :, k * TILE : (k + 1) * TILE] = rows[:, pl.ds(column, TILE)]

    keep_own = pltpu.make_async_copy(packed.at[me], own_all.at[me], keep_sem.at[1])
    keep_own.start()

    @pl.loop(1, lane)
    def _(hop):
        deal(z * lane + (inner + hop) % lane).start()

    @pl.loop(1, layers)
    def _(s):
        @pl.when(z - s >= 0)
        def _():
            pl.semaphore_wait(in_below.at[z - s], 1)

            @pl.when(above)
            def _():
                signal(in_below.at[z - s], up)

        @pl.when(z + s < layers)
        def _():
            pl.semaphore_wait(in_above.at[z + s], 1)

            @pl.when(below)
            def _():
                signal(in_above.at[z + s], down)

        for piece in range(pieces):
            @pl.when(z - s >= 0)
            def _():
                origin = at(z - s, y, core)
                arrived(origin, piece)

                @pl.when(z + 1 < layers)
                def _():
                    pass_on(0, origin, piece, up).start()

                if depth > 1:
                    pass_on(2, origin, piece, across).start()
                pass_on(3, origin, piece, twin).start()

            @pl.when(z + s < layers)
            def _():
                origin = at(z + s, y, core)
                arrived(origin, piece)

                @pl.when(z > 0)
                def _():
                    pass_on(1, origin, piece, down).start()

                if depth > 1:
                    pass_on(2, origin, piece, across).start()
                pass_on(3, origin, piece, twin).start()

        ahead, behind = layers - 1 - z, z

        @pl.loop(jnp.where(s == behind, 1, s), jnp.where(s >= behind, jnp.minimum(s, ahead) + 1, 0))
        def _(far):
            deals(z + far)

        @pl.loop(jnp.where(s == ahead, 1, s), jnp.where(s >= ahead, jnp.minimum(s, behind) + 1, 0))
        def _(far):
            deals(z - far)

    if depth > 1:
        @pl.loop(1, layers + 1)
        def _(s):
            for piece in range(pieces):
                @pl.when(z - s + 1 >= 0)
                def _():
                    origin = at(z - s + 1, depth - 1 - y, core)
                    arrived(origin, piece)
                    pass_on(3, origin, piece, twin).start()

                @pl.when(jnp.logical_and(s > 1, z + s - 1 < layers))
                def _():
                    origin = at(z + s - 1, depth - 1 - y, core)
                    arrived(origin, piece)
                    pass_on(3, origin, piece, twin).start()

    @pl.loop(0, layers)
    def _(layer):
        for side in range(depth):
            for piece in range(pieces):
                arrived(at(layer, side, CORES - 1 - core), piece)

    @pl.loop(1, n)
    def _(hop):
        peer = lax.rem(me + hop, n)
        pltpu.make_async_remote_copy(
            src_ref=packed.at[peer], dst_ref=own_all.at[peer], send_sem=own_send.at[peer],
            recv_sem=own_recv.at[peer], device_id={"row": peer}, device_id_type=MESH,
        ).wait()

    keep.wait()
    keep_own.wait()

    @pl.loop(0, layers)
    def _(layer):
        origin = at(layer, y, core)
        for piece in range(pieces):
            @pl.when(jnp.logical_and(layer <= z, z + 1 < layers))
            def _():
                pass_on(0, origin, piece, up).wait_send()

            @pl.when(jnp.logical_and(layer >= z, z > 0))
            def _():
                pass_on(1, origin, piece, down).wait_send()

            if depth > 1:
                pass_on(2, origin, piece, across).wait_send()
            for side in range(depth):
                pass_on(3, at(layer, side, core), piece, twin).wait_send()


def two(value):
    high = value.astype(jnp.bfloat16)
    return high, (value - high.astype(jnp.float32)).astype(jnp.bfloat16)


def dot(left, right, over=1):
    return lax.dot_general(
        left, right, (((over,), (0,)), ((), ())), preferred_element_type=jnp.float32
    )


def normal(slab_in, own_in, out_ref, arcs_buf, own_buf, slab_buf, out_buf, average, own_parts, in_sem, out_sem):
    total = own_in.shape[0]
    spans = [(at, min(STEP, SLAB - at)) for at in range(0, SLAB, STEP)]

    def load(step):
        at, wide = spans[step]
        columns = pl.ds(at, wide)
        return pltpu.make_async_copy(slab_in.at[:, columns], slab_buf.at[:, columns], in_sem.at[2 + step])

    def store(step):
        at, wide = spans[step]
        columns = pl.ds(at, wide)
        return pltpu.make_async_copy(out_buf.at[columns], out_ref.at[columns], out_sem.at[step])

    load_arcs = pltpu.make_async_copy(slab_in.at[:, pl.ds(SLAB, TILE)], arcs_buf, in_sem.at[0])
    load_own = pltpu.make_async_copy(own_in, own_buf, in_sem.at[1])
    load_arcs.start()
    load_own.start()
    for step in range(len(spans)):
        load(step).start()

    load_arcs.wait()
    arcs = arcs_buf[...]
    alike = (arcs[:, 0:1] == jnp.transpose(arcs)[0:1, :]).astype(jnp.float32)
    counts = jnp.sum(alike, axis=1, keepdims=True)
    average[...] = (alike / counts).astype(jnp.bfloat16)
    mask = alike.astype(jnp.bfloat16)
    load_own.wait()
    own = own_buf[...]
    high = own.astype(jnp.bfloat16)
    middle, low = two(own - high.astype(jnp.float32))
    sums = dot(mask, low) + dot(mask, middle) + dot(mask, high)
    high, low = two(own - sums / counts)
    own_parts[:total], own_parts[total : 2 * total], own_parts[2 * total :] = high, low, high

    for step, (at, wide) in enumerate(spans):
        load(step).wait()
        slab = slab_buf[:, at : at + wide]
        high, low = two(jnp.transpose(slab - dot(average[...], slab.astype(jnp.bfloat16))))
        out_buf[at : at + wide] = dot(jnp.concatenate([low, high, high], axis=1), own_parts[...])
        store(step).start()

    for step in range(len(spans)):
        store(step).wait()


def shards(depth, design_rows, arc_ids, tile_order):
    obs, columns = design_rows.shape
    n = lax.axis_size("row")
    mine = columns // n
    total = n * obs
    pieces = obs // ROWS * PARTS
    layers = n // (depth * CORES)
    slab_all, own_all = pl.pallas_call(
        functools.partial(exchange, depth),
        out_shape=(
            jax.ShapeDtypeStruct((n, obs, WIDE), jnp.float32),
            jax.ShapeDtypeStruct((n, obs, mine), jnp.float32),
        ),
        in_specs=[
            pl.BlockSpec(memory_space=pltpu.HBM),
            pl.BlockSpec(memory_space=pltpu.HBM),
            pl.BlockSpec(memory_space=pltpu.HBM),
        ],
        out_specs=(pl.BlockSpec(memory_space=pl.ANY), pl.BlockSpec(memory_space=pl.ANY)),
        scratch_shapes=[
            pltpu.SMEM(tile_order.shape, jnp.int32),
            pltpu.SMEM(arc_ids.shape, jnp.int32),
            pltpu.VMEM(design_rows.shape, jnp.float32),
            pltpu.VMEM((obs, WIDE), jnp.float32),
            pltpu.VMEM((n, obs, mine), jnp.float32),
            pltpu.SemaphoreType.DMA((n, pieces)),
            pltpu.SemaphoreType.DMA((n,)),
            pltpu.SemaphoreType.DMA((4, n, pieces)),
            pltpu.SemaphoreType.DMA((n,)),
            pltpu.SemaphoreType.DMA((3,)),
            pltpu.SemaphoreType.DMA((2,)),
            pltpu.SemaphoreType.REGULAR((layers,)),
            pltpu.SemaphoreType.REGULAR((layers,)),
        ],
        compiler_params=pltpu.CompilerParams(
            collective_id=0, has_side_effects=True, vmem_limit_bytes=60 << 20
        ),
        name="exchange",
    )(tile_order, arc_ids, design_rows)
    slab_all = slab_all.reshape(total, WIDE)
    own_all = own_all.reshape(total, mine)
    steps = pl.cdiv(SLAB, STEP)
    return pl.pallas_call(
        normal,
        out_shape=jax.ShapeDtypeStruct((SLAB, mine), jnp.float32),
        in_specs=[pl.BlockSpec(memory_space=pl.ANY), pl.BlockSpec(memory_space=pl.ANY)],
        out_specs=pl.BlockSpec(memory_space=pl.ANY),
        scratch_shapes=[
            pltpu.VMEM((total, TILE), jnp.float32),
            pltpu.VMEM((total, mine), jnp.float32),
            pltpu.VMEM((total, SLAB), jnp.float32),
            pltpu.VMEM((SLAB, mine), jnp.float32),
            pltpu.VMEM((total, total), jnp.bfloat16),
            pltpu.VMEM((3 * total, mine), jnp.bfloat16),
            pltpu.SemaphoreType.DMA((2 + steps,)),
            pltpu.SemaphoreType.DMA((steps,)),
        ],
        compiler_params=pltpu.CompilerParams(vmem_limit_bytes=60 << 20),
        name="normal",
    )(slab_all, own_all)


def solution(mesh):
    depth = 4 // mesh.shape["groups"]
    return jax.shard_map(
        functools.partial(shards, depth),
        mesh=mesh,
        in_specs=(P(("groups", "row"), None), P(("groups", "row")), P()),
        out_specs=P("groups", "row"),
        check_vma=False,
    )
```

```python
import functools

import jax
import jax.numpy as jnp
from jax import lax
from jax.experimental import pallas as pl
from jax.experimental.pallas import tpu as pltpu
from jax.sharding import PartitionSpec as P

SLAB = 2944
TILE = 128
WIDE = SLAB + TILE
STEP = 1152
PARTS = 1
ROWS = 8
CORES = 2
MESH = pl.DeviceIdType.MESH


def exchange(
    depth, order_in, ids_in, rows_in, slab_all, own_all,
    order, ids, rows, stage, packed, slab_recv, own_recv, slab_send, own_send, load_sem, keep_sem,
    in_below, in_above,
):
    me = lax.axis_index("row")
    n = lax.axis_size("row")
    obs = rows.shape[0]
    tiles = packed.shape[2] // TILE
    lane = depth * CORES
    layers = n // lane
    z, inner = me // lane, me % lane
    y, core = inner // CORES, inner % CORES
    halves, part = obs // ROWS, WIDE // PARTS
    pieces = halves * PARTS

    loads = [
        pltpu.make_async_copy(rows_in, rows, load_sem.at[0]),
        pltpu.make_async_copy(ids_in, ids, load_sem.at[1]),
        pltpu.make_async_copy(order_in, order, load_sem.at[2]),
    ]
    for load in loads:
        load.start()

    def at(layer, side, unit):
        return (layer * depth + side) * CORES + unit

    up, down = at(z + 1, y, core), at(z - 1, y, core)
    across, twin = at(z, depth - 1 - y, core), at(z, y, CORES - 1 - core)
    below, above = z > 0, z + 1 < layers

    def signal(semaphore, target):
        pl.semaphore_signal(semaphore, inc=1, device_id={"row": target}, device_id_type=MESH)

    barrier = pltpu.get_barrier_semaphore()

    @pl.loop(1, lane)
    def _(hop):
        signal(barrier, z * lane + (inner + hop) % lane)

    @pl.when(above)
    def _():
        signal(barrier, up)

    @pl.when(below)
    def _():
        signal(barrier, down)

    for load in loads:
        load.wait()
    stage[:, :SLAB] = rows[:, :SLAB]
    for obs_at in range(obs):
        value = ids[obs_at].astype(jnp.float32)
        stage[obs_at : obs_at + 1, SLAB:] = jnp.full((1, TILE), value, jnp.float32)

    def cut(ref, piece):
        return ref.at[pl.ds((piece // PARTS) * ROWS, ROWS), pl.ds((piece % PARTS) * part, part)]

    def pass_on(kind, origin, piece, target, own=False):
        return pltpu.make_async_remote_copy(
            src_ref=cut(stage if own else slab_all.at[origin], piece),
            dst_ref=cut(slab_all.at[origin], piece),
            send_sem=slab_send.at[kind, origin, piece],
            recv_sem=slab_recv.at[origin, piece],
            device_id={"row": target},
            device_id_type=MESH,
        )

    def arrived(origin, piece):
        pass_on(3, origin, piece, twin).wait_recv()

    def deal(peer):
        return pltpu.make_async_remote_copy(
            src_ref=packed.at[peer],
            dst_ref=own_all.at[me],
            send_sem=own_send.at[peer],
            recv_sem=own_recv.at[me],
            device_id={"row": peer},
            device_id_type=MESH,
        )

    def deals(layer):
        @pl.loop(0, lane)
        def _(unit):
            deal(layer * lane + unit).start()

    pl.semaphore_wait(barrier, lane - 1 + jnp.where(above, 1, 0) + jnp.where(below, 1, 0))

    @pl.when(above)
    def _():
        signal(in_below.at[z], up)

    @pl.when(below)
    def _():
        signal(in_above.at[z], down)

    for piece in range(pieces):
        @pl.when(z + 1 < layers)
        def _():
            pass_on(0, me, piece, up, True).start()

        @pl.when(z > 0)
        def _():
            pass_on(1, me, piece, down, True).start()

        if depth > 1:
            pass_on(2, me, piece, across, True).start()
        pass_on(3, me, piece, twin, True).start()
    keep = pltpu.make_async_copy(stage, slab_all.at[me], keep_sem.at[0])
    keep.start()

    @pl.loop(0, n)
    def _(peer):
        for k in range(tiles):
            column = order[peer * tiles + k] * TILE
            packed[peer, :, k * TILE : (k + 1) * TILE] = rows[:, pl.ds(column, TILE)]

    keep_own = pltpu.make_async_copy(packed.at[me], own_all.at[me], keep_sem.at[1])
    keep_own.start()

    @pl.loop(1, lane)
    def _(hop):
        deal(z * lane + (inner + hop) % lane).start()

    @pl.loop(1, layers)
    def _(s):
        @pl.when(z - s >= 0)
        def _():
            pl.semaphore_wait(in_below.at[z - s], 1)

            @pl.when(above)
            def _():
                signal(in_below.at[z - s], up)

        @pl.when(z + s < layers)
        def _():
            pl.semaphore_wait(in_above.at[z + s], 1)

            @pl.when(below)
            def _():
                signal(in_above.at[z + s], down)

        for piece in range(pieces):
            @pl.when(z - s >= 0)
            def _():
                origin = at(z - s, y, core)
                arrived(origin, piece)

                @pl.when(z + 1 < layers)
                def _():
                    pass_on(0, origin, piece, up).start()

                if depth > 1:
                    pass_on(2, origin, piece, across).start()
                pass_on(3, origin, piece, twin).start()

            @pl.when(z + s < layers)
            def _():
                origin = at(z + s, y, core)
                arrived(origin, piece)

                @pl.when(z > 0)
                def _():
                    pass_on(1, origin, piece, down).start()

                if depth > 1:
                    pass_on(2, origin, piece, across).start()
                pass_on(3, origin, piece, twin).start()

        ahead, behind = layers - 1 - z, z

        @pl.loop(jnp.where(s == behind, 1, s), jnp.where(s >= behind, jnp.minimum(s, ahead) + 1, 0))
        def _(far):
            deals(z + far)

        @pl.loop(jnp.where(s == ahead, 1, s), jnp.where(s >= ahead, jnp.minimum(s, behind) + 1, 0))
        def _(far):
            deals(z - far)

    if depth > 1:
        @pl.loop(1, layers + 1)
        def _(s):
            for piece in range(pieces):
                @pl.when(z - s + 1 >= 0)
                def _():
                    origin = at(z - s + 1, depth - 1 - y, core)
                    arrived(origin, piece)
                    pass_on(3, origin, piece, twin).start()

                @pl.when(jnp.logical_and(s > 1, z + s - 1 < layers))
                def _():
                    origin = at(z + s - 1, depth - 1 - y, core)
                    arrived(origin, piece)
                    pass_on(3, origin, piece, twin).start()

    @pl.loop(0, layers)
    def _(layer):
        for side in range(depth):
            for piece in range(pieces):
                arrived(at(layer, side, CORES - 1 - core), piece)

    @pl.loop(1, n)
    def _(hop):
        peer = lax.rem(me + hop, n)
        pltpu.make_async_remote_copy(
            src_ref=packed.at[peer], dst_ref=own_all.at[peer], send_sem=own_send.at[peer],
            recv_sem=own_recv.at[peer], device_id={"row": peer}, device_id_type=MESH,
        ).wait()

    keep.wait()
    keep_own.wait()

    @pl.loop(0, layers)
    def _(layer):
        origin = at(layer, y, core)
        for piece in range(pieces):
            @pl.when(jnp.logical_and(layer <= z, z + 1 < layers))
            def _():
                pass_on(0, origin, piece, up).wait_send()

            @pl.when(jnp.logical_and(layer >= z, z > 0))
            def _():
                pass_on(1, origin, piece, down).wait_send()

            if depth > 1:
                pass_on(2, origin, piece, across).wait_send()
            for side in range(depth):
                pass_on(3, at(layer, side, core), piece, twin).wait_send()


def two(value):
    high = value.astype(jnp.bfloat16)
    return high, (value - high.astype(jnp.float32)).astype(jnp.bfloat16)


def dot(left, right, over=1):
    return lax.dot_general(
        left, right, (((over,), (0,)), ((), ())), preferred_element_type=jnp.float32
    )


def normal(slab_in, own_in, out_ref, arcs_buf, own_buf, slab_buf, out_buf, average, own_parts, in_sem, out_sem):
    total = own_in.shape[0]
    spans = [(at, min(STEP, SLAB - at)) for at in range(0, SLAB, STEP)]

    def load(step):
        at, wide = spans[step]
        columns = pl.ds(at, wide)
        return pltpu.make_async_copy(slab_in.at[:, columns], slab_buf.at[:, columns], in_sem.at[2 + step])

    def store(step):
        at, wide = spans[step]
        columns = pl.ds(at, wide)
        return pltpu.make_async_copy(out_buf.at[columns], out_ref.at[columns], out_sem.at[step])

    load_arcs = pltpu.make_async_copy(slab_in.at[:, pl.ds(SLAB, TILE)], arcs_buf, in_sem.at[0])
    load_own = pltpu.make_async_copy(own_in, own_buf, in_sem.at[1])
    load_arcs.start()
    load_own.start()
    for step in range(len(spans)):
        load(step).start()

    load_arcs.wait()
    arcs = arcs_buf[...]
    alike = (arcs[:, 0:1] == jnp.transpose(arcs)[0:1, :]).astype(jnp.float32)
    counts = jnp.sum(alike, axis=1, keepdims=True)
    average[...] = (alike / counts).astype(jnp.bfloat16)
    mask = alike.astype(jnp.bfloat16)
    load_own.wait()
    own = own_buf[...]
    high = own.astype(jnp.bfloat16)
    middle, low = two(own - high.astype(jnp.float32))
    sums = dot(mask, low) + dot(mask, middle) + dot(mask, high)
    high, low = two(own - sums / counts)
    own_parts[:total], own_parts[total : 2 * total], own_parts[2 * total :] = high, low, high

    for step, (at, wide) in enumerate(spans):
        load(step).wait()
        slab = slab_buf[:, at : at + wide]
        high, low = two(jnp.transpose(slab - dot(average[...], slab.astype(jnp.bfloat16))))
        out_buf[at : at + wide] = dot(jnp.concatenate([low, high, high], axis=1), own_parts[...])
        store(step).start()

    for step in range(len(spans)):
        store(step).wait()


def shards(depth, design_rows, arc_ids, tile_order):
    obs, columns = design_rows.shape
    n = lax.axis_size("row")
    mine = columns // n
    total = n * obs
    pieces = obs // ROWS * PARTS
    layers = n // (depth * CORES)
    slab_all, own_all = pl.pallas_call(
        functools.partial(exchange, depth),
        out_shape=(
            jax.ShapeDtypeStruct((n, obs, WIDE), jnp.float32),
            jax.ShapeDtypeStruct((n, obs, mine), jnp.float32),
        ),
        in_specs=[
            pl.BlockSpec(memory_space=pltpu.HBM),
            pl.BlockSpec(memory_space=pltpu.HBM),
            pl.BlockSpec(memory_space=pltpu.HBM),
        ],
        out_specs=(pl.BlockSpec(memory_space=pl.ANY), pl.BlockSpec(memory_space=pl.ANY)),
        scratch_shapes=[
            pltpu.SMEM(tile_order.shape, jnp.int32),
            pltpu.SMEM(arc_ids.shape, jnp.int32),
            pltpu.VMEM(design_rows.shape, jnp.float32),
            pltpu.VMEM((obs, WIDE), jnp.float32),
            pltpu.VMEM((n, obs, mine), jnp.float32),
            pltpu.SemaphoreType.DMA((n, pieces)),
            pltpu.SemaphoreType.DMA((n,)),
            pltpu.SemaphoreType.DMA((4, n, pieces)),
            pltpu.SemaphoreType.DMA((n,)),
            pltpu.SemaphoreType.DMA((3,)),
            pltpu.SemaphoreType.DMA((2,)),
            pltpu.SemaphoreType.REGULAR((layers,)),
            pltpu.SemaphoreType.REGULAR((layers,)),
        ],
        compiler_params=pltpu.CompilerParams(
            collective_id=0, has_side_effects=True, vmem_limit_bytes=60 << 20
        ),
        name="exchange",
    )(tile_order, arc_ids, design_rows)
    slab_all = slab_all.reshape(total, WIDE)
    own_all = own_all.reshape(total, mine)
    steps = pl.cdiv(SLAB, STEP)
    return pl.pallas_call(
        normal,
        out_shape=jax.ShapeDtypeStruct((SLAB, mine), jnp.float32),
        in_specs=[pl.BlockSpec(memory_space=pl.ANY), pl.BlockSpec(memory_space=pl.ANY)],
        out_specs=pl.BlockSpec(memory_space=pl.ANY),
        scratch_shapes=[
            pltpu.VMEM((total, TILE), jnp.float32),
            pltpu.VMEM((total, mine), jnp.float32),
            pltpu.VMEM((total, SLAB), jnp.float32),
            pltpu.VMEM((SLAB, mine), jnp.float32),
            pltpu.VMEM((total, total), jnp.bfloat16),
            pltpu.VMEM((3 * total, mine), jnp.bfloat16),
            pltpu.SemaphoreType.DMA((2 + steps,)),
            pltpu.SemaphoreType.DMA((steps,)),
        ],
        compiler_params=pltpu.CompilerParams(vmem_limit_bytes=60 << 20),
        name="normal",
    )(slab_all, own_all)


def solution(mesh):
    depth = 4 // mesh.shape["groups"]
    return jax.shard_map(
        functools.partial(shards, depth),
        mesh=mesh,
        in_specs=(P(("groups", "row"), None), P(("groups", "row")), P()),
        out_specs=P("groups", "row"),
        check_vma=False,
    )
```
